32 devices in a mesh: wide: 8 (over z, y), narrow: 4 (over x, core).
Axes of the slice: x: 2, y: 2, z: 4, core: 2. Of those that a mesh axis runs over, the one named last changes fastest.
Arguments:
- fine_in: bfloat16 [32, 32, 64, 80], P(None, 'narrow', 'wide'), may hold values from -6 to 6
- voxel_mask: int32 [32, 64, 80], P('narrow', 'wide'), may hold values from 0 to 1, as said below
- timestep: int32 [1], replicated, may hold values from 0 to 999
- w_enc: bfloat16 [27, 32, 32], replicated, may hold values from -0.21875 to 0.21875
- b_enc: float32 [32], replicated, may hold values from -3 to 3
- w_down: bfloat16 [128, 256], replicated, may hold values from -0.375 to 0.375
- w_time: bfloat16 [128, 256], replicated, may hold values from -0.5 to 0.5
- w_coarse: bfloat16 [27, 128, 128], replicated, may hold values from -0.109375 to 0.109375
- b_coarse: float32 [128], replicated, may hold values from -3 to 3
- w_up: bfloat16 [32, 128], replicated, may hold values from -0.5 to 0.5
- w_dec: bfloat16 [27, 32, 64], replicated, may hold values from -0.15625 to 0.15625
- b_dec: float32 [32], replicated, may hold values from -3 to 3
Outputs:
- denoised: bfloat16 [32, 32, 64, 80], P(None, 'narrow', 'wide')
The draws below stay inside these ranges and needn't reach their ends.
Inputs may be any that keep to these rules, and one draw needn't show every extreme that they name: `voxel_mask`: each device's tile of 8 x 8 x 80 voxels consists of aligned 8 x 8 x 8 blocks; a block is active when it holds a 1. Two tiles with the same narrow index whose wide indices differ by 4 hold at most 10 active blocks together, and some such pair holds exactly 10.
All inputs are finite; a program needn't handle non-finite values.
Results may differ from the reference program's by a relative error of at most 0.0044.
Values may be sent and summed in bfloat16 or wider, within the bound.
A program may use at most 64 MiB of HBM per device.

```python
import math
import jax
import jax.numpy as jnp
from jax import lax

C = 32
CC = 128
TE = 128
TX = 8
TY = 8
Z = 80
NX = 32
NY = 64


def draw_voxel_mask(key, part):
    tiles_x = NX // TX
    tiles_y = NY // TY
    half_y = tiles_y // 2
    blocks_x = TX // 8
    blocks_y = TY // 8
    blocks_z = Z // 8
    per_tile = blocks_x * blocks_y * blocks_z
    keys = jax.random.split(jax.random.fold_in(key, 17), 7)
    heavy = jax.random.randint(keys[0], (tiles_x, half_y), 3 * per_tile // 4, per_tile + 1)
    chosen = jax.random.randint(keys[1], (), 0, tiles_x * half_y)
    places = jnp.arange(tiles_x * half_y, dtype=jnp.int32).reshape(tiles_x, half_y)
    heavy = jnp.where(places == chosen, per_tile, heavy)
    light = jax.random.randint(keys[2], (tiles_x, half_y), 0, per_tile - heavy + 1)
    sides = jax.random.randint(keys[3], (tiles_x, half_y), 0, 2)
    lower = jnp.where(sides == 0, heavy, light)
    upper = jnp.where(sides == 0, light, heavy)
    counts = jnp.concatenate([lower, upper], axis=1)
    scores = jax.random.randint(keys[4], (tiles_x, tiles_y, per_tile), 0, 1 << 20) * per_tile + jnp.arange(per_tile, dtype=jnp.int32)
    ranks = jnp.argsort(jnp.argsort(scores, axis=-1), axis=-1)
    active = (ranks < counts[..., None]).astype(jnp.int32)
    voxels = jax.random.randint(keys[5], (tiles_x, tiles_y, per_tile, 512), 0, 2)
    forced = jax.random.randint(keys[6], (tiles_x, tiles_y, per_tile), 0, 512)
    voxels = jnp.where(jnp.arange(512, dtype=jnp.int32) == forced[..., None], 1, voxels)
    filled = active[..., None] * voxels
    filled = filled.reshape(tiles_x, tiles_y, blocks_x, blocks_y, blocks_z, 8, 8, 8)
    filled = jnp.transpose(filled, (0, 2, 5, 1, 3, 6, 4, 7))
    return filled.reshape(NX, NY, Z).astype(jnp.int32)


def level_of(rng, dims, pieces, smallest, high):
    def one(axis_at, parts):
        steps = jax.random.uniform(jax.random.fold_in(jax.random.fold_in(rng, 6), axis_at), (parts,), jnp.float32, smallest / len(pieces), high / len(pieces))
        return jnp.repeat(jnp.exp(steps), dims[axis_at] // parts).reshape((-1,) + (1,) * (len(dims) - axis_at - 1))

    gain = one(*pieces[0])
    for cut in pieces[1:]:
        gain = gain * one(*cut)
    return gain


def bell_draw(own_key, shape, width, reach, pieces=(), kind=jnp.bfloat16):
    array = jax.random.normal(own_key, shape, jnp.float32) * width
    if len(pieces) > 0:
        array = level_of(own_key, shape, pieces, -0.22, 0.18) * array
    return jnp.clip(array, min=-reach, max=reach).astype(kind)


def setup_inputs(seed: int = 0) -> dict:
    seeds = jax.random.split(jax.random.key(seed), 13)
    return {
        "fine_in": bell_draw(seeds[0], (C, NX, NY, Z), 1.0, 6.0, ((1, 4), (2, 8))),
        "voxel_mask": draw_voxel_mask(jax.random.fold_in(seeds[12], 71), 0),
        "timestep": jax.random.randint(seeds[2], (1,), 0, 1000).astype(jnp.int32),
        "w_enc": bell_draw(seeds[3], (27, C, C), (27 * C) ** -0.5, 0.21875),
        "b_enc": bell_draw(seeds[4], (C,), 0.5, 3.0, (), jnp.float32),
        "w_down": bell_draw(seeds[5], (CC, 8 * C), (8 * C) ** -0.5, 0.375),
        "w_time": bell_draw(seeds[6], (TE, 2 * CC), TE ** -0.5, 0.5),
        "w_coarse": bell_draw(seeds[7], (27, CC, CC), (27 * CC) ** -0.5, 0.109375),
        "b_coarse": bell_draw(seeds[8], (CC,), 0.5, 3.0, (), jnp.float32),
        "w_up": bell_draw(seeds[9], (C, CC), CC ** -0.5, 0.5),
        "w_dec": bell_draw(seeds[10], (27, C, 2 * C), (54 * C) ** -0.5, 0.15625),
        "b_dec": bell_draw(seeds[11], (C,), 0.5, 3.0, (), jnp.float32),
    }


LAYOUT = ("NCDHW", "OIDHW", "NCDHW")


def cube_weight(weight):
    out_ch = weight.shape[1]
    in_ch = weight.shape[2]
    return jnp.transpose(weight.reshape(3, 3, 3, out_ch, in_ch), (3, 4, 0, 1, 2))


def conv_scene(field_in, weight):
    size_x = field_in.shape[1]
    size_y = field_in.shape[2]
    size_z = field_in.shape[3]
    kernel = cube_weight(weight).astype(jnp.float32)
    padded = jnp.pad(field_in, ((0, 0), (1, 1), (1, 1), (1, 1)))

    def slab_conv(offset):
        window = lax.dynamic_slice_in_dim(padded, offset, 10, 1).astype(jnp.float32)
        result = lax.conv_general_dilated(window[None], kernel, (1, 1, 1), "VALID", dimension_numbers=LAYOUT, precision=lax.Precision.HIGHEST, preferred_element_type=jnp.float32)
        return result[0]

    offsets = jnp.arange(size_x // 8, dtype=jnp.int32) * 8
    stacked = lax.map(slab_conv, offsets)
    return jnp.moveaxis(stacked, 0, 1).reshape(weight.shape[1], size_x, size_y, size_z)


def time_features(timestep, embed_width):
    halves = embed_width // 2
    freqs = jnp.exp(-math.log(10000.0) * jnp.arange(halves, dtype=jnp.float32) / halves)
    angles = timestep[0].astype(jnp.float32) * freqs
    return jnp.concatenate([jnp.sin(angles), jnp.cos(angles)]).astype(jnp.bfloat16)


def pool_children(field_in):
    chans = field_in.shape[0]
    half_x = field_in.shape[1] // 2
    half_y = field_in.shape[2] // 2
    half_z = field_in.shape[3] // 2
    grouped = field_in.reshape(chans, half_x, 2, half_y, 2, half_z, 2)
    return jnp.transpose(grouped, (2, 4, 6, 0, 1, 3, 5)).reshape(8 * chans, half_x, half_y, half_z)


def coarse_mask(mask_in):
    half_x = mask_in.shape[0] // 2
    half_y = mask_in.shape[1] // 2
    half_z = mask_in.shape[2] // 2
    return jnp.max(mask_in.reshape(half_x, 2, half_y, 2, half_z, 2), axis=(1, 3, 5)) > 0


def upsample(field_in):
    return jnp.repeat(jnp.repeat(jnp.repeat(field_in, 2, axis=1), 2, axis=2), 2, axis=3)


def reference(fine_in, voxel_mask, timestep, w_enc, b_enc, w_down, w_time, w_coarse, b_coarse, w_up, w_dec, b_dec):
    active = voxel_mask[None] > 0
    masked = jnp.where(active, fine_in, jnp.zeros_like(fine_in))
    encoded = jnp.where(active, jax.nn.silu(conv_scene(masked, w_enc) + b_enc[:, None, None, None]), 0.0).astype(jnp.bfloat16)
    pooled = pool_children(encoded)
    coarse_on = coarse_mask(voxel_mask)[None]
    embedded = time_features(timestep, w_time.shape[0])
    film = jnp.dot(embedded[None], w_time, preferred_element_type=jnp.float32)[0]
    chans = w_down.shape[0]
    gains = 1.0 + film[:chans]
    shifts = film[chans:]
    lifted = jnp.dot(w_down, pooled.reshape(pooled.shape[0], -1), preferred_element_type=jnp.float32)
    lifted = lifted.reshape((chans,) + pooled.shape[1:])
    coarse_in = jnp.where(coarse_on, jax.nn.silu(lifted * gains[:, None, None, None] + shifts[:, None, None, None]), 0.0).astype(jnp.bfloat16)
    coarse_act = jnp.where(coarse_on, jax.nn.silu(conv_scene(coarse_in, w_coarse) + b_coarse[:, None, None, None]), 0.0).astype(jnp.bfloat16)
    lifted_up = jnp.dot(w_up, coarse_act.reshape(chans, -1), preferred_element_type=jnp.float32)
    lifted_up = lifted_up.reshape((w_up.shape[0],) + coarse_act.shape[1:]).astype(jnp.bfloat16)
    joined = jnp.concatenate([encoded, upsample(lifted_up)], axis=0)
    decoded = conv_scene(joined, w_dec) + b_dec[:, None, None, None]
    return jnp.where(active, decoded, 0.0).astype(jnp.bfloat16)
```

```python
import functools
import math

import jax
import jax.numpy as jnp
from jax import lax
from jax.experimental import pallas as pl
from jax.experimental.pallas import tpu as pltpu
from jax.sharding import PartitionSpec as P

BF = jnp.bfloat16
F32 = jnp.float32
LANES = 128
WAYS = [(1, 0), (-1, 0), (0, 1), (0, -1), (1, 1), (1, -1), (-1, 1), (-1, -1)]
NT = (((1,), (1,)), ((), ()))


def round_up(n, m):
    return -(-n // m) * m


def time_features(timestep, embed_width):
    halves = embed_width // 2
    freqs = jnp.exp(-math.log(10000.0) * jnp.arange(halves, dtype=F32) / halves)
    angles = timestep[0].astype(F32) * freqs
    return jnp.concatenate([jnp.sin(angles), jnp.cos(angles)]).astype(BF)


def silu(v):
    return v / (1.0 + jnp.exp(-v))


def edge(step, size, landing):
    if step == 0:
        return pl.ds(1, size)
    if landing:
        return pl.ds(0 if step == 1 else size + 1, 1)
    return pl.ds(size if step == 1 else 1, 1)


def fine_kernel(
    n_narrow, n_wide,
    fine_ref, mask_ref, rows_ref, cols_ref, w_enc_ref, w_down_ref, w_coarse_ref, w_up_ref, w_dec_ref,
    out_ref,
    masked, enc, coarse, lift, on_keep, mask_keep, turn, acc, k_enc, k_dec_e, k_dec_l, k_down,
    send_sem, recv_sem,
):
    chans, tx, ty, tz = fine_ref.shape
    cx, cy = tx // 2, ty // 2
    kz = coarse.shape[2]
    zl = masked.shape[3]
    cc = w_up_ref.shape[1]
    ni, wi = lax.axis_index("narrow"), lax.axis_index("wide")

    def there(dx, dy):
        ok = None
        for pos, step, size in ((ni, dx, n_narrow), (wi, dy, n_wide)):
            if step == 1:
                one = pos < size - 1
            elif step == -1:
                one = pos > 0
            else:
                continue
            ok = one if ok is None else jnp.logical_and(ok, one)
        return ok

    def copy(phase, buf, way):
        dx, dy = WAYS[way]
        sx, sy = buf.shape[0] - 2, buf.shape[1] - 2
        return pltpu.make_async_remote_copy(
            src_ref=buf.at[edge(dx, sx, False), edge(dy, sy, False)],
            dst_ref=buf.at[edge(dx, sx, True), edge(dy, sy, True)],
            send_sem=send_sem.at[phase, way],
            recv_sem=recv_sem.at[phase, way],
            device_id={"narrow": ni + dx, "wide": wi + dy},
            device_id_type=pl.DeviceIdType.MESH,
        )

    def send(phase, buf):
        for way, (dx, dy) in enumerate(WAYS):
            @pl.when(there(dx, dy))
            def _():
                copy(phase, buf, way).start()

    def arrive(phase, buf):
        for way, (dx, dy) in enumerate(WAYS):
            @pl.when(there(-dx, -dy))
            def _():
                copy(phase, buf, way).wait_recv()

    def sent(phase, buf):
        for way, (dx, dy) in enumerate(WAYS):
            @pl.when(there(dx, dy))
            def _():
                copy(phase, buf, way).wait_send()

    for buf in (masked, enc, coarse, lift):
        sx, sy = buf.shape[0], buf.shape[1]
        for at in (0, sx - 1):
            buf[at] = jnp.zeros(buf.shape[1:], BF)
        for at in (0, sy - 1):
            buf[:, at] = jnp.zeros((sx,) + buf.shape[2:], BF)

    barrier = pltpu.get_barrier_semaphore()
    for dx, dy in WAYS:
        @pl.when(there(dx, dy))
        def _():
            pl.semaphore_signal(
                barrier, inc=1, device_id={"narrow": ni + dx, "wide": wi + dy},
                device_id_type=pl.DeviceIdType.MESH,
            )

    turn[...] = jnp.zeros(turn.shape, F32)
    mask_keep[...] = jnp.zeros(mask_keep.shape, F32)
    mask_keep[:, :, 0:tz] = mask_ref[...].astype(F32)

    @pl.loop(0, tx)
    def _(x):
        tile = fine_ref[:, x].astype(F32)
        tile = jnp.where(mask_ref[x][None] > 0, tile, 0.0)
        turn[x, :, 0:tz] = tile.reshape(chans * ty, tz)
        for y in range(ty):
            masked[1 + x, 1 + y] = turn[x, pl.ds(y, chans, stride=ty), :].astype(BF)

    across = 1 + (ni > 0).astype(jnp.int32) + (ni < n_narrow - 1).astype(jnp.int32)
    along = 1 + (wi > 0).astype(jnp.int32) + (wi < n_wide - 1).astype(jnp.int32)
    pl.semaphore_wait(barrier, across * along - 1)
    send(0, masked)

    for ref in (k_enc, k_dec_e, k_dec_l):
        ref[...] = jnp.zeros(ref.shape, BF)
    m3 = 3 * chans
    for a in range(3):
        for b in range(3):
            tap = 9 * a + 3 * b
            we = w_enc_ref[tap:tap + 3].reshape(m3, chans)
            wd = w_dec_ref[tap:tap + 3].reshape(m3, 2 * chans)
            for dx in range(2):
                rows = slice(dx * m3, dx * m3 + m3)
                at = ((a + dx) * 3 + b) * chans
                k_enc[rows, at:at + chans] = we
                k_dec_e[rows, at:at + chans] = wd[:, 0:chans]
                k_dec_l[rows, at:at + chans] = wd[:, chans:]
    for a in range(2):
        for b in range(2):
            for c in range(2):
                src = (4 * a + 2 * b + c) * chans
                dst = (4 * c + 2 * a + b) * chans
                k_down[:, dst:dst + chans] = w_down_ref[:, src:src + chans]

    row = lax.broadcasted_iota(jnp.int32, (kz, zl), 0)
    lane = lax.broadcasted_iota(jnp.int32, (kz, zl), 1)
    inside = lane < tz
    even = jnp.logical_and(lane == 2 * row, inside).astype(F32)
    odd = jnp.logical_and(lane == 2 * row + 1, inside).astype(F32)
    picks = jnp.concatenate([even, odd], axis=0).astype(BF)
    spread = (even + odd).astype(BF)

    def gather_fine(buf, x2, y0):
        parts = []
        for a in range(4):
            for b in range(3):
                parts.append(jnp.concatenate([buf[2 * x2 + a, y0 + b], buf[2 * x2 + a, y0 + 1 + b]], axis=1))
        return jnp.concatenate(parts, axis=0)

    def gather_lift(x2, y0):
        parts = []
        for a in range(4):
            for b in range(3):
                xa = x2 + (a + 1) // 2
                parts.append(jnp.concatenate(
                    [lift[xa, (y0 + b + 1) // 2], lift[xa, (y0 + b + 2) // 2]], axis=1))
        return jnp.concatenate(parts, axis=0)

    def fold(part, dx, dy):
        r = part[dx * m3:(dx + 1) * m3, dy * zl:(dy + 1) * zl]
        return (pltpu.roll(r[0:chans], 1, 1) + r[chans:2 * chans]
                + pltpu.roll(r[2 * chans:], zl - 1, 1))

    arrive(0, masked)

    @pl.loop(0, cx)
    def _(x2):
        for y0 in range(0, ty, 2):
            part = jnp.dot(k_enc[...], gather_fine(masked, x2, y0), preferred_element_type=F32)
            for dx in range(2):
                for dy in range(2):
                    v = silu(fold(part, dx, dy) + cols_ref[0:chans])
                    m = mask_keep[2 * x2 + dx, y0 + dy:y0 + dy + 1, :]
                    enc[1 + 2 * x2 + dx, 1 + y0 + dy] = jnp.where(m > 0, v, 0.0).astype(BF)

    send(1, enc)

    gains, shifts, b_coarse = rows_ref[0:1], rows_ref[1:2], rows_ref[2:3]

    @pl.loop(0, cx)
    def _(x2):
        for y2 in range(cy):
            block = enc[pl.ds(1 + 2 * x2, 2), 1 + 2 * y2:3 + 2 * y2].reshape(4 * chans, zl)
            both = lax.dot_general(picks, block, NT, preferred_element_type=F32).astype(BF)
            pooled = jnp.concatenate([both[0:kz], both[kz:]], axis=1)
            lifted = lax.dot_general(pooled, k_down[...], NT, preferred_element_type=F32)
            two = mask_keep[2 * x2, 2 * y2:2 * y2 + 2] + mask_keep[2 * x2 + 1, 2 * y2:2 * y2 + 2]
            four = jnp.broadcast_to(jnp.sum(two, axis=0, keepdims=True), (cc, zl)).astype(BF)
            on = lax.dot_general(spread, four, NT, preferred_element_type=F32)
            on_keep[x2, y2] = on
            v = silu(lifted * gains + shifts)
            coarse[1 + x2, 1 + y2] = jnp.where(on > 0, v, 0.0).astype(BF)

    send(2, coarse)
    arrive(2, coarse)

    halves = 2 if cx % 2 == 0 else 1

    @pl.loop(0, cx // halves)
    def _(x2):
        x2 = x2 * halves
        taps, weights = [], []
        for a in range(3):
            for b in range(3):
                taps.append(coarse[pl.ds(x2 + a, halves), b:b + cy].reshape(halves * cy * kz, cc))
                tap = 9 * a + 3 * b
                weights.append(w_coarse_ref[tap:tap + 3].reshape(3 * cc, cc))
        r = lax.dot_general(jnp.concatenate(taps, axis=1), jnp.concatenate(weights, axis=1), NT,
                            preferred_element_type=F32)
        n = halves * cy * kz
        v = pltpu.roll(r[:, 0:cc], 1, 0) + r[:, cc:2 * cc] + pltpu.roll(r[:, 2 * cc:], n - 1, 0)
        on = on_keep[pl.ds(x2, halves)].reshape(n, cc)
        act = jnp.where(on > 0, silu(v + b_coarse), 0.0).astype(BF)
        for h in range(halves):
            for y2 in range(cy):
                at = (h * cy + y2) * kz
                up = lax.dot_general(w_up_ref[...], act[at:at + kz], NT, preferred_element_type=F32).astype(BF)
                lift[1 + x2 + h, 1 + y2] = jnp.dot(up, spread, preferred_element_type=F32).astype(BF)

    send(3, lift)
    arrive(1, enc)

    @pl.loop(0, cx)
    def _(x2):
        for y0 in range(0, ty, 2):
            acc[x2, y0 // 2] = jnp.dot(k_dec_e[...], gather_fine(enc, x2, y0), preferred_element_type=F32)

    arrive(3, lift)

    @pl.loop(0, cx)
    def _(x2):
        for y0 in range(0, ty, 2):
            part = acc[x2, y0 // 2] + jnp.dot(
                k_dec_l[...], gather_lift(x2, y0), preferred_element_type=F32)
            for dx in range(2):
                for dy in range(2):
                    v = fold(part, dx, dy) + cols_ref[chans:2 * chans]
                    turn[2 * x2 + dx, pl.ds(y0 + dy, chans, stride=ty), :] = v
        for dx in range(2):
            tile = turn[2 * x2 + dx].reshape(chans, ty, zl)[:, :, 0:tz]
            tile = jnp.where(mask_ref[2 * x2 + dx][None] > 0, tile, 0.0)
            out_ref[:, 2 * x2 + dx] = tile.astype(BF)

    for phase, buf in enumerate((masked, enc, coarse, lift)):
        sent(phase, buf)


def on_device(n_narrow, n_wide, fine_in, voxel_mask, timestep, w_enc, b_enc, w_down, w_time,
              w_coarse, b_coarse, w_up, w_dec, b_dec):
    chans, tx, ty, tz = fine_in.shape
    cc = w_down.shape[0]
    zl = round_up(tz + 1, LANES)
    kz = round_up(tz // 2 + 1, 16)
    embedded = time_features(timestep, w_time.shape[0])
    film = jnp.dot(embedded[None], w_time, preferred_element_type=F32)[0]
    rows = jnp.stack([1.0 + film[:cc], film[cc:], b_coarse])
    cols = jnp.broadcast_to(jnp.concatenate([b_enc, b_dec])[:, None], (2 * chans, zl))
    k_rows, k_cols = 6 * chans, 12 * chans
    vmem = pl.BlockSpec(memory_space=pltpu.VMEM)
    return pl.pallas_call(
        functools.partial(fine_kernel, n_narrow, n_wide),
        out_shape=jax.ShapeDtypeStruct(fine_in.shape, BF),
        in_specs=[vmem] * 9,
        out_specs=vmem,
        scratch_shapes=[
            pltpu.VMEM((tx + 2, ty + 2, chans, zl), BF),
            pltpu.VMEM((tx + 2, ty + 2, chans, zl), BF),
            pltpu.VMEM((tx // 2 + 2, ty // 2 + 2, kz, cc), BF),
            pltpu.VMEM((tx // 2 + 2, ty // 2 + 2, chans, zl), BF),
            pltpu.VMEM((tx // 2, ty // 2, kz, cc), F32),
            pltpu.VMEM((tx, ty, zl), F32),
            pltpu.VMEM((tx, chans * ty, zl), F32),
            pltpu.VMEM((tx // 2, ty // 2, k_rows, 2 * zl), F32),
            pltpu.VMEM((k_rows, k_cols), BF),
            pltpu.VMEM((k_rows, k_cols), BF),
            pltpu.VMEM((k_rows, k_cols), BF),
            pltpu.VMEM((cc, 8 * chans), BF),
            pltpu.SemaphoreType.DMA((4, len(WAYS))),
            pltpu.SemaphoreType.DMA((4, len(WAYS))),
        ],
        compiler_params=pltpu.CompilerParams(
            collective_id=0, has_side_effects=True, vmem_limit_bytes=48 * 1024 * 1024
        ),
    )(fine_in, voxel_mask, rows, cols, w_enc, w_down, w_coarse, w_up, w_dec)


def solution(mesh):
    return jax.shard_map(
        functools.partial(on_device, mesh.shape["narrow"], mesh.shape["wide"]),
        mesh=mesh,
        in_specs=(
            P(None, "narrow", "wide", None),
            P("narrow", "wide", None),
            P(), P(), P(), P(), P(), P(), P(), P(), P(), P(),
        ),
        out_specs=P(None, "narrow", "wide", None),
        check_vma=False,
    )
```

```python
import functools
import math

import jax
import jax.numpy as jnp
from jax import lax
from jax.experimental import pallas as pl
from jax.experimental.pallas import tpu as pltpu
from jax.sharding import PartitionSpec as P

BF = jnp.bfloat16
F32 = jnp.float32
LANES = 128
WAYS = [(1, 0), (-1, 0), (0, 1), (0, -1), (1, 1), (1, -1), (-1, 1), (-1, -1)]
NT = (((1,), (1,)), ((), ()))
TN = (((0,), (0,)), ((), ()))


def round_up(n, m):
    return -(-n // m) * m


def reduced(angle):
    turns = jnp.floor(angle * (0.5 / math.pi) + 0.5)
    r = angle - turns * 6.28125
    r = r - turns * 0.0019350051879882812
    return r - turns * 3.019916037e-07


def series(square, first):
    total = jnp.zeros_like(square)
    for power in range(first + 20, first - 1, -2):
        total = total * square + (-1.0) ** (power // 2) / math.factorial(power)
    return total


def features(step_ref, width):
    halves = width // 2
    at = lax.broadcasted_iota(jnp.int32, (8, width), 1)
    k = jnp.where(at < halves, at, at - halves).astype(F32)
    r = reduced(step_ref[0].astype(F32) * jnp.exp(-math.log(10000.0) * k / halves))
    q = r * r
    return jnp.where(at < halves, r * series(q, 1), series(q, 0)).astype(BF)


def silu(v):
    return v / (1.0 + jnp.exp(-v))


def edge(step, size, landing):
    if step == 0:
        return pl.ds(1, size)
    if landing:
        return pl.ds(0 if step == 1 else size + 1, 1)
    return pl.ds(size if step == 1 else 1, 1)


def fine_kernel(
    n_narrow, n_wide,
    step_ref, *refs
):
    inputs, refs = refs[:11], refs[11:]
    out_ref, refs = refs[0], refs[1:]
    local, refs = refs[:11], refs[11:]
    loads = [pltpu.make_async_copy(a, b, refs[-1].at[i]) for i, (a, b) in enumerate(zip(inputs, local))]
    for load in loads:
        load.start()
    (fine_ref, mask_ref, w_enc_ref, w_down_ref, w_dec_ref, w_time_ref, b_enc_ref, b_dec_ref,
     b_coarse_ref, w_up_ref, w_coarse_ref) = local
    (masked, enc, coarse, lift, flat, y_out, side_x, side_y, on_keep, mask_keep, turn, acc, k_enc, k_dec_e, k_dec_l, k_down,
     send_sem, recv_sem, _) = refs
    chans, tx, ty, tz = fine_ref.shape
    cx, cy = tx // 2, ty // 2
    kz = coarse.shape[2]
    zl = masked.shape[3]
    cc = w_up_ref.shape[1]
    ni, wi = lax.axis_index("narrow"), lax.axis_index("wide")

    def there(dx, dy):
        ok = None
        for pos, step, size in ((ni, dx, n_narrow), (wi, dy, n_wide)):
            if step == 1:
                one = pos < size - 1
            elif step == -1:
                one = pos > 0
            else:
                continue
            ok = one if ok is None else jnp.logical_and(ok, one)
        return ok

    def copy(phase, buf, way):
        dx, dy = WAYS[way]
        sx, sy = buf.shape[0] - 2, buf.shape[1] - 2
        src = buf.at[edge(dx, sx, False), edge(dy, sy, False)]
        dst = buf.at[edge(dx, sx, True), edge(dy, sy, True)]
        if phase == 3 and dy == 0:
            src, dst = flat.at[cx - 1 if dx == 1 else 0], side_x.at[0 if dx == 1 else 1]
        elif phase == 3 and dx == 0:
            src, dst = y_out.at[1 if dy == 1 else 0], side_y.at[0 if dy == 1 else 1]
        return pltpu.make_async_remote_copy(
            src_ref=src,
            dst_ref=dst,
            send_sem=send_sem.at[phase, way],
            recv_sem=recv_sem.at[phase, way],
            device_id={"narrow": ni + dx, "wide": wi + dy},
            device_id_type=pl.DeviceIdType.MESH,
        )

    def send(phase, buf):
        for way, (dx, dy) in enumerate(WAYS):
            @pl.when(there(dx, dy))
            def _():
                copy(phase, buf, way).start()

    def arrive(phase, buf):
        for way, (dx, dy) in enumerate(WAYS):
            @pl.when(there(-dx, -dy))
            def _():
                copy(phase, buf, way).wait_recv()

    def sent(phase, buf):
        for way, (dx, dy) in enumerate(WAYS):
            @pl.when(there(dx, dy))
            def _():
                copy(phase, buf, way).wait_send()

    for buf in (masked, enc, coarse):
        sx, sy = buf.shape[0], buf.shape[1]
        for at in (0, sx - 1):
            buf[at] = jnp.zeros(buf.shape[1:], BF)
        for at in (0, sy - 1):
            buf[:, at] = jnp.zeros((sx,) + buf.shape[2:], BF)

    for buf in (side_x, side_y):
        buf[...] = jnp.zeros(buf.shape, BF)
    for at_x in (0, cx + 1):
        for at_y in (0, cy + 1):
            lift[at_x, at_y] = jnp.zeros(lift.shape[2:], BF)

    barrier = pltpu.get_barrier_semaphore()
    for dx, dy in WAYS:
        @pl.when(there(dx, dy))
        def _():
            pl.semaphore_signal(
                barrier, inc=1, device_id={"narrow": ni + dx, "wide": wi + dy},
                device_id_type=pl.DeviceIdType.MESH,
            )

    turn[...] = jnp.zeros(turn.shape, F32)
    loads[0].wait()
    loads[1].wait()
    mask_keep[...] = jnp.zeros(mask_keep.shape, F32)
    mask_keep[:, :, 0:tz] = mask_ref[...].astype(F32)

    @pl.loop(0, tx)
    def _(x):
        tile = fine_ref[:, x].astype(F32)
        tile = jnp.where(mask_ref[x][None] > 0, tile, 0.0)
        turn[x, :, 0:tz] = tile.reshape(chans * ty, tz)
        for y in range(ty):
            masked[1 + x, 1 + y] = turn[x, pl.ds(y, chans, stride=ty), :].astype(BF)

    across = 1 + (ni > 0).astype(jnp.int32) + (ni < n_narrow - 1).astype(jnp.int32)
    along = 1 + (wi > 0).astype(jnp.int32) + (wi < n_wide - 1).astype(jnp.int32)
    pl.semaphore_wait(barrier, across * along - 1)
    send(0, masked)
    for load in loads[2:10]:
        load.wait()

    for ref in (k_enc, k_dec_e, k_dec_l):
        ref[...] = jnp.zeros(ref.shape, BF)
    m3 = 3 * chans
    for a in range(3):
        for b in range(3):
            tap = 9 * a + 3 * b
            we = w_enc_ref[tap:tap + 3].reshape(m3, chans)
            wd = w_dec_ref[tap:tap + 3].reshape(m3, 2 * chans)
            for dx in range(2):
                rows = slice(dx * m3, dx * m3 + m3)
                at = ((a + dx) * 3 + b) * chans
                k_enc[rows, at:at + chans] = we
                k_dec_e[rows, at:at + chans] = wd[:, 0:chans]
                k_dec_l[rows, at:at + chans] = wd[:, chans:]
    for a in range(2):
        for b in range(2):
            for c in range(2):
                src = (4 * a + 2 * b + c) * chans
                dst = (4 * c + 2 * a + b) * chans
                k_down[:, dst:dst + chans] = w_down_ref[:, src:src + chans]

    row = lax.broadcasted_iota(jnp.int32, (kz, zl), 0)
    lane = lax.broadcasted_iota(jnp.int32, (kz, zl), 1)
    inside = lane < tz
    even = jnp.logical_and(lane == 2 * row, inside).astype(F32)
    odd = jnp.logical_and(lane == 2 * row + 1, inside).astype(F32)
    picks = jnp.concatenate([even, odd], axis=0).astype(BF)
    spread = (even + odd).astype(BF)

    eye = (lax.broadcasted_iota(jnp.int32, (chans, chans), 0)
           == lax.broadcasted_iota(jnp.int32, (chans, chans), 1))

    def column(ref):
        return jnp.broadcast_to(
            jnp.sum(jnp.where(eye, ref[...], 0.0), axis=1, keepdims=True), (chans, zl))

    b_enc, b_dec = column(b_enc_ref), column(b_dec_ref)

    def gather_fine(buf, x2, y0):
        parts = []
        for a in range(4):
            for b in range(3):
                parts.append(jnp.concatenate([buf[2 * x2 + a, y0 + b], buf[2 * x2 + a, y0 + 1 + b]], axis=1))
        return jnp.concatenate(parts, axis=0)

    def gather_lift(x2, y0):
        parts = []
        for a in range(4):
            for b in range(3):
                xa = x2 + (a + 1) // 2
                parts.append(jnp.concatenate(
                    [lift[xa, (y0 + b + 1) // 2], lift[xa, (y0 + b + 2) // 2]], axis=1))
        return jnp.concatenate(parts, axis=0)

    def fold(part, dx, dy):
        r = part[dx * m3:(dx + 1) * m3, dy * zl:(dy + 1) * zl]
        return (pltpu.roll(r[0:chans], 1, 1) + r[chans:2 * chans]
                + pltpu.roll(r[2 * chans:], zl - 1, 1))

    arrive(0, masked)

    @pl.loop(0, cx)
    def _(x2):
        for y0 in range(0, ty, 2):
            part = jnp.dot(k_enc[...], gather_fine(masked, x2, y0), preferred_element_type=F32)
            for dx in range(2):
                for dy in range(2):
                    v = silu(fold(part, dx, dy) + b_enc)
                    m = mask_keep[2 * x2 + dx, y0 + dy:y0 + dy + 1, :]
                    enc[1 + 2 * x2 + dx, 1 + y0 + dy] = jnp.where(m > 0, v, 0.0).astype(BF)

    film = jnp.dot(features(step_ref, w_time_ref.shape[0]), w_time_ref[...], preferred_element_type=F32)
    gains, shifts = 1.0 + film[0:1, 0:cc], film[0:1, cc:]
    b_coarse = b_coarse_ref[...]

    @pl.loop(0, cx)
    def _(x2):
        for y2 in range(cy):
            block = enc[pl.ds(1 + 2 * x2, 2), 1 + 2 * y2:3 + 2 * y2].reshape(4 * chans, zl)
            both = lax.dot_general(picks, block, NT, preferred_element_type=F32).astype(BF)
            pooled = jnp.concatenate([both[0:kz], both[kz:]], axis=1)
            lifted = lax.dot_general(pooled, k_down[...], NT, preferred_element_type=F32)
            two = mask_keep[2 * x2, 2 * y2:2 * y2 + 2] + mask_keep[2 * x2 + 1, 2 * y2:2 * y2 + 2]
            four = jnp.broadcast_to(jnp.sum(two, axis=0, keepdims=True), (cc, zl)).astype(BF)
            on = lax.dot_general(spread, four, NT, preferred_element_type=F32)
            on_keep[x2, y2] = on
            v = silu(lifted * gains + shifts)
            coarse[1 + x2, 1 + y2] = jnp.where(on > 0, v, 0.0).astype(BF)

    send(2, coarse)
    loads[10].wait()
    arrive(2, coarse)
    send(1, enc)

    halves = 2 if cx % 2 == 0 else 1

    @pl.loop(0, cx // halves)
    def _(x2):
        x2 = x2 * halves
        taps, weights = [], []
        for a in range(3):
            for b in range(3):
                taps.append(coarse[pl.ds(x2 + a, halves), b:b + cy].reshape(halves * cy * kz, cc))
                tap = 9 * a + 3 * b
                weights.append(w_coarse_ref[tap:tap + 3].reshape(3 * cc, cc))
        r = lax.dot_general(jnp.concatenate(taps, axis=1), jnp.concatenate(weights, axis=1), NT,
                            preferred_element_type=F32)
        n = halves * cy * kz
        v = pltpu.roll(r[:, 0:cc], 1, 0) + r[:, cc:2 * cc] + pltpu.roll(r[:, 2 * cc:], n - 1, 0)
        on = on_keep[pl.ds(x2, halves)].reshape(n, cc)
        act = jnp.where(on > 0, silu(v + b_coarse), 0.0).astype(BF)
        up = lax.dot_general(act, w_up_ref[...], NT, preferred_element_type=F32).astype(BF)
        for h in range(halves):
            for y2 in range(cy):
                at = (h * cy + y2) * kz
                flat[x2 + h, :, y2 * chans:(y2 + 1) * chans] = up[at:at + kz]

    def raise_z(columns, count):
        wide = lax.dot_general(columns, spread, TN, preferred_element_type=F32)
        return wide.astype(BF).reshape(count, chans, zl)

    for x2 in range(cx):
        for at, y2 in enumerate((0, cy - 1)):
            y_out[at, :, x2 * chans:(x2 + 1) * chans] = flat[x2, :, y2 * chans:(y2 + 1) * chans]
        lift[1 + x2, 1:1 + cy] = raise_z(flat[x2], cy)
    send(3, lift)
    arrive(1, enc)

    @pl.loop(0, cx)
    def _(x2):
        for y0 in range(0, ty, 2):
            acc[x2, y0 // 2] = jnp.dot(k_dec_e[...], gather_fine(enc, x2, y0), preferred_element_type=F32)

    arrive(3, lift)
    for at, edge_at in enumerate((0, cx + 1)):
        lift[edge_at, 1:1 + cy] = raise_z(side_x[at], cy)
    for at, edge_at in enumerate((0, cy + 1)):
        lift[1:1 + cx, edge_at] = raise_z(side_y[at], cx)

    @pl.loop(0, cx)
    def _(x2):
        for y0 in range(0, ty, 2):
            part = acc[x2, y0 // 2] + jnp.dot(
                k_dec_l[...], gather_lift(x2, y0), preferred_element_type=F32)
            for dx in range(2):
                for dy in range(2):
                    v = fold(part, dx, dy) + b_dec
                    turn[2 * x2 + dx, pl.ds(y0 + dy, chans, stride=ty), :] = v
        for dx in range(2):
            tile = turn[2 * x2 + dx].reshape(chans, ty, zl)[:, :, 0:tz]
            tile = jnp.where(mask_ref[2 * x2 + dx][None] > 0, tile, 0.0)
            out_ref[:, 2 * x2 + dx] = tile.astype(BF)

    for phase, buf in enumerate((masked, enc, coarse, lift)):
        sent(phase, buf)


def on_device(n_narrow, n_wide, fine_in, voxel_mask, timestep, w_enc, b_enc, w_down, w_time,
              w_coarse, b_coarse, w_up, w_dec, b_dec):
    chans, tx, ty, tz = fine_in.shape
    cc = w_down.shape[0]
    zl = round_up(tz + 1, LANES)
    kz = round_up(tz // 2 + 1, 16)
    inputs = (fine_in, voxel_mask, w_enc, w_down, w_dec, w_time, b_enc[None], b_dec[None],
              b_coarse[None], w_up, w_coarse)
    k_rows, k_cols = 6 * chans, 12 * chans
    vmem = pl.BlockSpec(memory_space=pltpu.VMEM)
    return pl.pallas_call(
        functools.partial(fine_kernel, n_narrow, n_wide),
        out_shape=jax.ShapeDtypeStruct(fine_in.shape, BF),
        in_specs=[pl.BlockSpec(memory_space=pltpu.SMEM)]
        + [pl.BlockSpec(memory_space=pltpu.HBM)] * len(inputs),
        out_specs=vmem,
        scratch_shapes=[pltpu.VMEM(a.shape, a.dtype) for a in inputs] + [
            pltpu.VMEM((tx + 2, ty + 2, chans, zl), BF),
            pltpu.VMEM((tx + 2, ty + 2, chans, zl), BF),
            pltpu.VMEM((tx // 2 + 2, ty // 2 + 2, kz, cc), BF),
            pltpu.VMEM((tx // 2 + 2, ty // 2 + 2, chans, zl), BF),
            pltpu.VMEM((tx // 2, kz, ty // 2 * chans), BF),
            pltpu.VMEM((2, kz, tx // 2 * chans), BF),
            pltpu.VMEM((2, kz, ty // 2 * chans), BF),
            pltpu.VMEM((2, kz, tx // 2 * chans), BF),
            pltpu.VMEM((tx // 2, ty // 2, kz, cc), F32),
            pltpu.VMEM((tx, ty, zl), F32),
            pltpu.VMEM((tx, chans * ty, zl), F32),
            pltpu.VMEM((tx // 2, ty // 2, k_rows, 2 * zl), F32),
            pltpu.VMEM((k_rows, k_cols), BF),
            pltpu.VMEM((k_rows, k_cols), BF),
            pltpu.VMEM((k_rows, k_cols), BF),
            pltpu.VMEM((cc, 8 * chans), BF),
            pltpu.SemaphoreType.DMA((4, len(WAYS))),
            pltpu.SemaphoreType.DMA((4, len(WAYS))),
            pltpu.SemaphoreType.DMA((len(inputs),)),
        ],
        compiler_params=pltpu.CompilerParams(
            collective_id=0, has_side_effects=True, vmem_limit_bytes=48 * 1024 * 1024
        ),
    )(timestep, *inputs)


def solution(mesh):
    return jax.shard_map(
        functools.partial(on_device, mesh.shape["narrow"], mesh.shape["wide"]),
        mesh=mesh,
        in_specs=(
            P(None, "narrow", "wide", None),
            P("narrow", "wide", None),
            P(), P(), P(), P(), P(), P(), P(), P(), P(), P(),
        ),
        out_specs=P(None, "narrow", "wide", None),
        check_vma=False,
    )
```

```python
import functools
import math

import jax
import jax.numpy as jnp
from jax import lax
from jax.experimental import pallas as pl
from jax.experimental.pallas import tpu as pltpu
from jax.sharding import PartitionSpec as P

BF = jnp.bfloat16
F32 = jnp.float32
LANES = 128
WAYS = [(1, 0), (-1, 0), (0, 1), (0, -1), (1, 1), (1, -1), (-1, 1), (-1, -1)]
NT = (((1,), (1,)), ((), ()))
TN = (((0,), (0,)), ((), ()))


def round_up(n, m):
    return -(-n // m) * m


def reduced(angle):
    turns = jnp.floor(angle * (0.5 / math.pi) + 0.5)
    r = angle - turns * 6.28125
    r = r - turns * 0.0019350051879882812
    return r - turns * 3.019916037e-07


def series(square, first):
    total = jnp.zeros_like(square)
    for power in range(first + 20, first - 1, -2):
        total = total * square + (-1.0) ** (power // 2) / math.factorial(power)
    return total


def features(step_ref, width):
    halves = width // 2
    at = lax.broadcasted_iota(jnp.int32, (8, width), 1)
    k = jnp.where(at < halves, at, at - halves).astype(F32)
    r = reduced(step_ref[0].astype(F32) * jnp.exp(-math.log(10000.0) * k / halves))
    q = r * r
    return jnp.where(at < halves, r * series(q, 1), series(q, 0)).astype(BF)


def silu(v):
    return v / (1.0 + jnp.exp(-v))


def edge(step, size, landing):
    if step == 0:
        return pl.ds(1, size)
    if landing:
        return pl.ds(0 if step == 1 else size + 1, 1)
    return pl.ds(size if step == 1 else 1, 1)


def fine_kernel(
    n_narrow, n_wide,
    step_ref, *refs
):
    inputs, refs = refs[:11], refs[11:]
    out_ref, refs = refs[0], refs[1:]
    local, refs = refs[:11], refs[11:]
    loads = [pltpu.make_async_copy(a, b, refs[-1].at[i]) for i, (a, b) in enumerate(zip(inputs, local))]
    for load in loads:
        load.start()
    (fine_ref, mask_ref, w_enc_ref, w_down_ref, w_dec_ref, w_time_ref, b_enc_ref, b_dec_ref,
     b_coarse_ref, w_up_ref, w_coarse_ref) = local
    (masked, enc, coarse, lift, flat, y_out, side_x, side_y, on_keep, mask_keep, turn, acc, k_enc, k_dec_e, k_dec_l, k_down,
     send_sem, recv_sem, _) = refs
    chans, tx, ty, tz = fine_ref.shape
    cx, cy = tx // 2, ty // 2
    kz = coarse.shape[2]
    zl = masked.shape[3]
    cc = w_up_ref.shape[1]
    ni, wi = lax.axis_index("narrow"), lax.axis_index("wide")

    def there(dx, dy):
        ok = None
        for pos, step, size in ((ni, dx, n_narrow), (wi, dy, n_wide)):
            if step == 1:
                one = pos < size - 1
            elif step == -1:
                one = pos > 0
            else:
                continue
            ok = one if ok is None else jnp.logical_and(ok, one)
        return ok

    def copy(phase, buf, way):
        dx, dy = WAYS[way]
        sx, sy = buf.shape[0] - 2, buf.shape[1] - 2
        src = buf.at[edge(dx, sx, False), edge(dy, sy, False)]
        dst = buf.at[edge(dx, sx, True), edge(dy, sy, True)]
        if phase == 3 and dy == 0:
            src, dst = flat.at[cx - 1 if dx == 1 else 0], side_x.at[0 if dx == 1 else 1]
        elif phase == 3 and dx == 0:
            src, dst = y_out.at[1 if dy == 1 else 0], side_y.at[0 if dy == 1 else 1]
        return pltpu.make_async_remote_copy(
            src_ref=src,
            dst_ref=dst,
            send_sem=send_sem.at[phase, way],
            recv_sem=recv_sem.at[phase, way],
            device_id={"narrow": ni + dx, "wide": wi + dy},
            device_id_type=pl.DeviceIdType.MESH,
        )

    def send(phase, buf):
        for way, (dx, dy) in enumerate(WAYS):
            @pl.when(there(dx, dy))
            def _():
                copy(phase, buf, way).start()

    def arrive(phase, buf):
        for way, (dx, dy) in enumerate(WAYS):
            @pl.when(there(-dx, -dy))
            def _():
                copy(phase, buf, way).wait_recv()

    def sent(phase, buf):
        for way, (dx, dy) in enumerate(WAYS):
            @pl.when(there(dx, dy))
            def _():
                copy(phase, buf, way).wait_send()

    for buf in (masked, enc, coarse):
        sx, sy = buf.shape[0], buf.shape[1]
        for at in (0, sx - 1):
            buf[at] = jnp.zeros(buf.shape[1:], BF)
        for at in (0, sy - 1):
            buf[:, at] = jnp.zeros((sx,) + buf.shape[2:], BF)

    for buf in (side_x, side_y):
        buf[...] = jnp.zeros(buf.shape, BF)
    for at_x in (0, cx + 1):
        for at_y in (0, cy + 1):
            lift[at_x, at_y] = jnp.zeros(lift.shape[2:], BF)

    barrier = pltpu.get_barrier_semaphore()
    for dx, dy in WAYS:
        @pl.when(there(dx, dy))
        def _():
            pl.semaphore_signal(
                barrier, inc=1, device_id={"narrow": ni + dx, "wide": wi + dy},
                device_id_type=pl.DeviceIdType.MESH,
            )

    turn[...] = jnp.zeros(turn.shape, F32)
    loads[0].wait()
    loads[1].wait()
    mask_keep[...] = jnp.zeros(mask_keep.shape, F32)
    mask_keep[:, :, 0:tz] = mask_ref[...].astype(F32)

    @pl.loop(0, tx)
    def _(x):
        tile = fine_ref[:, x].astype(F32)
        tile = jnp.where(mask_ref[x][None] > 0, tile, 0.0)
        turn[x, :, 0:tz] = tile.reshape(chans * ty, tz)
        for y in range(ty):
            masked[1 + x, 1 + y] = turn[x, pl.ds(y, chans, stride=ty), :].astype(BF)

    across = 1 + (ni > 0).astype(jnp.int32) + (ni < n_narrow - 1).astype(jnp.int32)
    along = 1 + (wi > 0).astype(jnp.int32) + (wi < n_wide - 1).astype(jnp.int32)
    pl.semaphore_wait(barrier, across * along - 1)
    send(0, masked)
    for load in loads[2:10]:
        load.wait()

    for ref in (k_enc, k_dec_e, k_dec_l):
        ref[...] = jnp.zeros(ref.shape, BF)
    m3 = 3 * chans
    for a in range(3):
        for b in range(3):
            tap = 9 * a + 3 * b
            we = w_enc_ref[tap:tap + 3].reshape(m3, chans)
            wd = w_dec_ref[tap:tap + 3].reshape(m3, 2 * chans)
            for dx in range(2):
                rows = slice(dx * m3, dx * m3 + m3)
                at = ((a + dx) * 3 + b) * chans
                k_enc[rows, at:at + chans] = we
                k_dec_e[rows, at:at + chans] = wd[:, 0:chans]
                k_dec_l[rows, at:at + chans] = wd[:, chans:]
    for a in range(2):
        for b in range(2):
            for c in range(2):
                src = (4 * a + 2 * b + c) * chans
                dst = (4 * c + 2 * a + b) * chans
                k_down[:, dst:dst + chans] = w_down_ref[:, src:src + chans]

    row = lax.broadcasted_iota(jnp.int32, (kz, zl), 0)
    lane = lax.broadcasted_iota(jnp.int32, (kz, zl), 1)
    inside = lane < tz
    even = jnp.logical_and(lane == 2 * row, inside).astype(F32)
    odd = jnp.logical_and(lane == 2 * row + 1, inside).astype(F32)
    picks = jnp.concatenate([even, odd], axis=0).astype(BF)
    spread = (even + odd).astype(BF)

    eye = (lax.broadcasted_iota(jnp.int32, (chans, chans), 0)
           == lax.broadcasted_iota(jnp.int32, (chans, chans), 1))

    def column(ref):
        return jnp.broadcast_to(
            jnp.sum(jnp.where(eye, ref[...], 0.0), axis=1, keepdims=True), (chans, zl))

    b_enc, b_dec = column(b_enc_ref), column(b_dec_ref)

    def gather_fine(buf, x2, y0):
        parts = []
        for a in range(4):
            for b in range(3):
                parts.append(jnp.concatenate([buf[2 * x2 + a, y0 + b], buf[2 * x2 + a, y0 + 1 + b]], axis=1))
        return jnp.concatenate(parts, axis=0)

    def gather_lift(x2, y0):
        parts = []
        for a in range(4):
            for b in range(3):
                xa = x2 + (a + 1) // 2
                parts.append(jnp.concatenate(
                    [lift[xa, (y0 + b + 1) // 2], lift[xa, (y0 + b + 2) // 2]], axis=1))
        return jnp.concatenate(parts, axis=0)

    def fold(part, dx, dy):
        r = part[dx * m3:(dx + 1) * m3, dy * zl:(dy + 1) * zl]
        return (pltpu.roll(r[0:chans], 1, 1) + r[chans:2 * chans]
                + pltpu.roll(r[2 * chans:], zl - 1, 1))

    def inner(work):
        @pl.loop(1, cx - 1)
        def _(x2):
            for y0 in range(2, ty - 2, 2):
                work(x2, y0)

    def outer(work):
        @pl.loop(1, cx - 1)
        def _(x2):
            for y0 in (0, ty - 2):
                work(x2, y0)

        @pl.loop(0, 2)
        def _(end):
            for y0 in range(0, ty, 2):
                work(end * (cx - 1), y0)

    def encode(x2, y0):
        part = jnp.dot(k_enc[...], gather_fine(masked, x2, y0), preferred_element_type=F32)
        for dx in range(2):
            for dy in range(2):
                v = silu(fold(part, dx, dy) + b_enc)
                m = mask_keep[2 * x2 + dx, y0 + dy:y0 + dy + 1, :]
                enc[1 + 2 * x2 + dx, 1 + y0 + dy] = jnp.where(m > 0, v, 0.0).astype(BF)

    def decode_enc(x2, y0):
        acc[x2, y0 // 2] = jnp.dot(k_dec_e[...], gather_fine(enc, x2, y0), preferred_element_type=F32)

    inner(encode)
    arrive(0, masked)
    outer(encode)

    film = jnp.dot(features(step_ref, w_time_ref.shape[0]), w_time_ref[...], preferred_element_type=F32)
    gains, shifts = 1.0 + film[0:1, 0:cc], film[0:1, cc:]
    b_coarse = b_coarse_ref[...]

    @pl.loop(0, cx)
    def _(x2):
        for y2 in range(cy):
            block = enc[pl.ds(1 + 2 * x2, 2), 1 + 2 * y2:3 + 2 * y2].reshape(4 * chans, zl)
            both = lax.dot_general(picks, block, NT, preferred_element_type=F32).astype(BF)
            pooled = jnp.concatenate([both[0:kz], both[kz:]], axis=1)
            lifted = lax.dot_general(pooled, k_down[...], NT, preferred_element_type=F32)
            two = mask_keep[2 * x2, 2 * y2:2 * y2 + 2] + mask_keep[2 * x2 + 1, 2 * y2:2 * y2 + 2]
            four = jnp.broadcast_to(jnp.sum(two, axis=0, keepdims=True), (cc, zl)).astype(BF)
            on = lax.dot_general(spread, four, NT, preferred_element_type=F32)
            on_keep[x2, y2] = on
            v = silu(lifted * gains + shifts)
            coarse[1 + x2, 1 + y2] = jnp.where(on > 0, v, 0.0).astype(BF)

    send(2, coarse)
    inner(decode_enc)
    loads[10].wait()
    arrive(2, coarse)
    send(1, enc)

    halves = 2 if cx % 2 == 0 else 1

    @pl.loop(0, cx // halves)
    def _(x2):
        x2 = x2 * halves
        taps, weights = [], []
        for a in range(3):
            for b in range(3):
                taps.append(coarse[pl.ds(x2 + a, halves), b:b + cy].reshape(halves * cy * kz, cc))
                tap = 9 * a + 3 * b
                weights.append(w_coarse_ref[tap:tap + 3].reshape(3 * cc, cc))
        r = lax.dot_general(jnp.concatenate(taps, axis=1), jnp.concatenate(weights, axis=1), NT,
                            preferred_element_type=F32)
        n = halves * cy * kz
        v = pltpu.roll(r[:, 0:cc], 1, 0) + r[:, cc:2 * cc] + pltpu.roll(r[:, 2 * cc:], n - 1, 0)
        on = on_keep[pl.ds(x2, halves)].reshape(n, cc)
        act = jnp.where(on > 0, silu(v + b_coarse), 0.0).astype(BF)
        up = lax.dot_general(act, w_up_ref[...], NT, preferred_element_type=F32).astype(BF)
        for h in range(halves):
            for y2 in range(cy):
                at = (h * cy + y2) * kz
                flat[x2 + h, :, y2 * chans:(y2 + 1) * chans] = up[at:at + kz]

    def raise_z(columns, count):
        wide = lax.dot_general(columns, spread, TN, preferred_element_type=F32)
        return wide.astype(BF).reshape(count, chans, zl)

    for x2 in range(cx):
        for at, y2 in enumerate((0, cy - 1)):
            y_out[at, :, x2 * chans:(x2 + 1) * chans] = flat[x2, :, y2 * chans:(y2 + 1) * chans]
        lift[1 + x2, 1:1 + cy] = raise_z(flat[x2], cy)
    send(3, lift)
    arrive(1, enc)
    outer(decode_enc)

    arrive(3, lift)
    for at, edge_at in enumerate((0, cx + 1)):
        lift[edge_at, 1:1 + cy] = raise_z(side_x[at], cy)
    for at, edge_at in enumerate((0, cy + 1)):
        lift[1:1 + cx, edge_at] = raise_z(side_y[at], cx)

    @pl.loop(0, cx)
    def _(x2):
        for y0 in range(0, ty, 2):
            part = acc[x2, y0 // 2] + jnp.dot(
                k_dec_l[...], gather_lift(x2, y0), preferred_element_type=F32)
            for dx in range(2):
                for dy in range(2):
                    v = fold(part, dx, dy) + b_dec
                    turn[2 * x2 + dx, pl.ds(y0 + dy, chans, stride=ty), :] = v
        for dx in range(2):
            tile = turn[2 * x2 + dx].reshape(chans, ty, zl)[:, :, 0:tz]
            tile = jnp.where(mask_ref[2 * x2 + dx][None] > 0, tile, 0.0)
            out_ref[:, 2 * x2 + dx] = tile.astype(BF)

    for phase, buf in enumerate((masked, enc, coarse, lift)):
        sent(phase, buf)


def on_device(n_narrow, n_wide, fine_in, voxel_mask, timestep, w_enc, b_enc, w_down, w_time,
              w_coarse, b_coarse, w_up, w_dec, b_dec):
    chans, tx, ty, tz = fine_in.shape
    cc = w_down.shape[0]
    zl = round_up(tz + 1, LANES)
    kz = round_up(tz // 2 + 1, 16)
    inputs = (fine_in, voxel_mask, w_enc, w_down, w_dec, w_time, b_enc[None], b_dec[None],
              b_coarse[None], w_up, w_coarse)
    k_rows, k_cols = 6 * chans, 12 * chans
    vmem = pl.BlockSpec(memory_space=pltpu.VMEM)
    return pl.pallas_call(
        functools.partial(fine_kernel, n_narrow, n_wide),
        out_shape=jax.ShapeDtypeStruct(fine_in.shape, BF),
        in_specs=[pl.BlockSpec(memory_space=pltpu.SMEM)]
        + [pl.BlockSpec(memory_space=pltpu.HBM)] * len(inputs),
        out_specs=vmem,
        scratch_shapes=[pltpu.VMEM(a.shape, a.dtype) for a in inputs] + [
            pltpu.VMEM((tx + 2, ty + 2, chans, zl), BF),
            pltpu.VMEM((tx + 2, ty + 2, chans, zl), BF),
            pltpu.VMEM((tx // 2 + 2, ty // 2 + 2, kz, cc), BF),
            pltpu.VMEM((tx // 2 + 2, ty // 2 + 2, chans, zl), BF),
            pltpu.VMEM((tx // 2, kz, ty // 2 * chans), BF),
            pltpu.VMEM((2, kz, tx // 2 * chans), BF),
            pltpu.VMEM((2, kz, ty // 2 * chans), BF),
            pltpu.VMEM((2, kz, tx // 2 * chans), BF),
            pltpu.VMEM((tx // 2, ty // 2, kz, cc), F32),
            pltpu.VMEM((tx, ty, zl), F32),
            pltpu.VMEM((tx, chans * ty, zl), F32),
            pltpu.VMEM((tx // 2, ty // 2, k_rows, 2 * zl), F32),
            pltpu.VMEM((k_rows, k_cols), BF),
            pltpu.VMEM((k_rows, k_cols), BF),
            pltpu.VMEM((k_rows, k_cols), BF),
            pltpu.VMEM((cc, 8 * chans), BF),
            pltpu.SemaphoreType.DMA((4, len(WAYS))),
            pltpu.SemaphoreType.DMA((4, len(WAYS))),
            pltpu.SemaphoreType.DMA((len(inputs),)),
        ],
        compiler_params=pltpu.CompilerParams(
            collective_id=0, has_side_effects=True, vmem_limit_bytes=63 * 1024 * 1024
        ),
    )(timestep, *inputs)


def solution(mesh):
    return jax.shard_map(
        functools.partial(on_device, mesh.shape["narrow"], mesh.shape["wide"]),
        mesh=mesh,
        in_specs=(
            P(None, "narrow", "wide", None),
            P("narrow", "wide", None),
            P(), P(), P(), P(), P(), P(), P(), P(), P(), P(),
        ),
        out_specs=P(None, "narrow", "wide", None),
        check_vma=False,
    )
```

```python
import functools
import math

import jax
import jax.numpy as jnp
from jax import lax
from jax.experimental import pallas as pl
from jax.experimental.pallas import tpu as pltpu
from jax.sharding import PartitionSpec as P

BF = jnp.bfloat16
F32 = jnp.float32
LANES = 128
WAYS = [(1, 0), (-1, 0), (0, 1), (0, -1), (1, 1), (1, -1), (-1, 1), (-1, -1)]
NT = (((1,), (1,)), ((), ()))
TN = (((0,), (0,)), ((), ()))


def round_up(n, m):
    return -(-n // m) * m


def reduced(angle):
    turns = jnp.floor(angle * (0.5 / math.pi) + 0.5)
    r = angle - turns * 6.28125
    r = r - turns * 0.0019350051879882812
    return r - turns * 3.019916037e-07


def series(square, first):
    total = jnp.zeros_like(square)
    for power in range(first + 20, first - 1, -2):
        total = total * square + (-1.0) ** (power // 2) / math.factorial(power)
    return total


def features(step_ref, width):
    halves = width // 2
    at = lax.broadcasted_iota(jnp.int32, (8, width), 1)
    k = jnp.where(at < halves, at, at - halves).astype(F32)
    r = reduced(step_ref[0].astype(F32) * jnp.exp(-math.log(10000.0) * k / halves))
    q = r * r
    return jnp.where(at < halves, r * series(q, 1), series(q, 0)).astype(BF)


def silu(v):
    return v / (1.0 + jnp.exp(-v))


def edge(step, size, landing):
    if step == 0:
        return pl.ds(1, size)
    if landing:
        return pl.ds(0 if step == 1 else size + 1, 1)
    return pl.ds(size if step == 1 else 1, 1)


def fine_kernel(
    n_narrow, n_wide,
    step_ref, *refs
):
    inputs, refs = refs[:11], refs[11:]
    out_ref, refs = refs[0], refs[1:]
    local, refs = refs[:11], refs[11:]
    loads = [pltpu.make_async_copy(a, b, refs[-1].at[i]) for i, (a, b) in enumerate(zip(inputs, local))]
    for load in loads:
        load.start()
    (fine_ref, mask_ref, w_enc_ref, w_down_ref, w_dec_ref, w_time_ref, b_enc_ref, b_dec_ref,
     b_coarse_ref, w_up_ref, w_coarse_ref) = local
    (masked, enc, coarse, lift, flat, y_out, side_x, side_y, on_keep, mask_keep, turn, acc, k_enc, k_dec_e, k_dec_l, k_down,
     send_sem, recv_sem, _) = refs
    chans, tx, ty, tz = fine_ref.shape
    cx, cy = tx // 2, ty // 2
    kz = coarse.shape[2]
    zl = masked.shape[3]
    cc = w_up_ref.shape[1]
    ni, wi = lax.axis_index("narrow"), lax.axis_index("wide")

    def there(dx, dy):
        ok = None
        for pos, step, size in ((ni, dx, n_narrow), (wi, dy, n_wide)):
            if step == 1:
                one = pos < size - 1
            elif step == -1:
                one = pos > 0
            else:
                continue
            ok = one if ok is None else jnp.logical_and(ok, one)
        return ok

    def copy(phase, buf, way):
        dx, dy = WAYS[way]
        sx, sy = buf.shape[0] - 2, buf.shape[1] - 2
        src = buf.at[edge(dx, sx, False), edge(dy, sy, False)]
        dst = buf.at[edge(dx, sx, True), edge(dy, sy, True)]
        if phase == 3 and dy == 0:
            src, dst = flat.at[cx - 1 if dx == 1 else 0], side_x.at[0 if dx == 1 else 1]
        elif phase == 3 and dx == 0:
            src, dst = y_out.at[1 if dy == 1 else 0], side_y.at[0 if dy == 1 else 1]
        return pltpu.make_async_remote_copy(
            src_ref=src,
            dst_ref=dst,
            send_sem=send_sem.at[phase, way],
            recv_sem=recv_sem.at[phase, way],
            device_id={"narrow": ni + dx, "wide": wi + dy},
            device_id_type=pl.DeviceIdType.MESH,
        )

    def send(phase, buf):
        for way, (dx, dy) in enumerate(WAYS):
            @pl.when(there(dx, dy))
            def _():
                copy(phase, buf, way).start()

    def arrive(phase, buf):
        for way, (dx, dy) in enumerate(WAYS):
            @pl.when(there(-dx, -dy))
            def _():
                copy(phase, buf, way).wait_recv()

    def sent(phase, buf):
        for way, (dx, dy) in enumerate(WAYS):
            @pl.when(there(dx, dy))
            def _():
                copy(phase, buf, way).wait_send()

    for buf in (masked, enc, coarse):
        sx, sy = buf.shape[0], buf.shape[1]
        for at in (0, sx - 1):
            buf[at] = jnp.zeros(buf.shape[1:], BF)
        for at in (0, sy - 1):
            buf[:, at] = jnp.zeros((sx,) + buf.shape[2:], BF)

    for buf in (side_x, side_y):
        buf[...] = jnp.zeros(buf.shape, BF)
    for at_x in (0, cx + 1):
        for at_y in (0, cy + 1):
            lift[at_x, at_y] = jnp.zeros(lift.shape[2:], BF)

    barrier = pltpu.get_barrier_semaphore()
    for dx, dy in WAYS:
        @pl.when(there(dx, dy))
        def _():
            pl.semaphore_signal(
                barrier, inc=1, device_id={"narrow": ni + dx, "wide": wi + dy},
                device_id_type=pl.DeviceIdType.MESH,
            )

    turn[...] = jnp.zeros(turn.shape, F32)
    loads[0].wait()
    loads[1].wait()
    mask_keep[...] = jnp.zeros(mask_keep.shape, F32)
    mask_keep[:, :, 0:tz] = mask_ref[...].astype(F32)

    @pl.loop(0, tx)
    def _(x):
        tile = fine_ref[:, x].astype(F32)
        tile = jnp.where(mask_ref[x][None] > 0, tile, 0.0)
        turn[x, :, 0:tz] = tile.reshape(chans * ty, tz)
        for y in range(ty):
            masked[1 + x, 1 + y] = turn[x, pl.ds(y, chans, stride=ty), :].astype(BF)

    across = 1 + (ni > 0).astype(jnp.int32) + (ni < n_narrow - 1).astype(jnp.int32)
    along = 1 + (wi > 0).astype(jnp.int32) + (wi < n_wide - 1).astype(jnp.int32)
    pl.semaphore_wait(barrier, across * along - 1)
    send(0, masked)
    for load in loads[2:10]:
        load.wait()

    for ref in (k_enc, k_dec_e, k_dec_l):
        ref[...] = jnp.zeros(ref.shape, BF)
    m3 = 3 * chans
    for a in range(3):
        for b in range(3):
            tap = 9 * a + 3 * b
            we = w_enc_ref[tap:tap + 3].reshape(m3, chans)
            wd = w_dec_ref[tap:tap + 3].reshape(m3, 2 * chans)
            for dx in range(2):
                rows = slice(dx * m3, dx * m3 + m3)
                at = ((a + dx) * 3 + b) * chans
                k_enc[rows, at:at + chans] = we
                k_dec_e[rows, at:at + chans] = wd[:, 0:chans]
                k_dec_l[rows, at:at + chans] = wd[:, chans:]
    for a in range(2):
        for b in range(2):
            for c in range(2):
                src = (4 * a + 2 * b + c) * chans
                dst = (4 * c + 2 * a + b) * chans
                k_down[:, dst:dst + chans] = w_down_ref[:, src:src + chans]

    row = lax.broadcasted_iota(jnp.int32, (kz, zl), 0)
    lane = lax.broadcasted_iota(jnp.int32, (kz, zl), 1)
    inside = lane < tz
    even = jnp.logical_and(lane == 2 * row, inside).astype(F32)
    odd = jnp.logical_and(lane == 2 * row + 1, inside).astype(F32)
    picks = jnp.concatenate([even, odd], axis=0).astype(BF)
    spread = (even + odd).astype(BF)

    eye = (lax.broadcasted_iota(jnp.int32, (chans, chans), 0)
           == lax.broadcasted_iota(jnp.int32, (chans, chans), 1))

    def column(ref):
        return jnp.broadcast_to(
            jnp.sum(jnp.where(eye, ref[...], 0.0), axis=1, keepdims=True), (chans, zl))

    b_enc, b_dec = column(b_enc_ref), column(b_dec_ref)

    def gather_fine(buf, x2, y0):
        parts = []
        for a in range(4):
            for b in range(3):
                parts.append(jnp.concatenate([buf[2 * x2 + a, y0 + b], buf[2 * x2 + a, y0 + 1 + b]], axis=1))
        return jnp.concatenate(parts, axis=0)

    def gather_lift(x2, y0):
        parts = []
        for a in range(4):
            for b in range(3):
                xa = x2 + (a + 1) // 2
                parts.append(jnp.concatenate(
                    [lift[xa, (y0 + b + 1) // 2], lift[xa, (y0 + b + 2) // 2]], axis=1))
        return jnp.concatenate(parts, axis=0)

    def fold(part, dx, dy):
        r = part[dx * m3:(dx + 1) * m3, dy * zl:(dy + 1) * zl]
        return (pltpu.roll(r[0:chans], 1, 1) + r[chans:2 * chans]
                + pltpu.roll(r[2 * chans:], zl - 1, 1))

    def inner(work):
        @pl.loop(1, cx - 1)
        def _(x2):
            for y0 in range(2, ty - 2, 2):
                work(x2, y0)

    def outer(work):
        @pl.loop(1, cx - 1)
        def _(x2):
            for y0 in (0, ty - 2):
                work(x2, y0)

        @pl.loop(0, 2)
        def _(end):
            for y0 in range(0, ty, 2):
                work(end * (cx - 1), y0)

    def encode(x2, y0):
        part = jnp.dot(k_enc[...], gather_fine(masked, x2, y0), preferred_element_type=F32)
        for dx in range(2):
            for dy in range(2):
                v = silu(fold(part, dx, dy) + b_enc)
                m = mask_keep[2 * x2 + dx, y0 + dy:y0 + dy + 1, :]
                enc[1 + 2 * x2 + dx, 1 + y0 + dy] = jnp.where(m > 0, v, 0.0).astype(BF)

    def decode_enc(x2, y0):
        acc[x2, y0 // 2] = jnp.dot(k_dec_e[...], gather_fine(enc, x2, y0), preferred_element_type=F32)

    inner(encode)
    arrive(0, masked)
    outer(encode)

    film = jnp.dot(features(step_ref, w_time_ref.shape[0]), w_time_ref[...], preferred_element_type=F32)
    gains, shifts = 1.0 + film[0:1, 0:cc], film[0:1, cc:]
    b_coarse = b_coarse_ref[...]

    @pl.loop(0, cx)
    def _(x2):
        for y2 in range(cy):
            block = enc[pl.ds(1 + 2 * x2, 2), 1 + 2 * y2:3 + 2 * y2].reshape(4 * chans, zl)
            both = lax.dot_general(picks, block, NT, preferred_element_type=F32).astype(BF)
            pooled = jnp.concatenate([both[0:kz], both[kz:]], axis=1)
            lifted = lax.dot_general(pooled, k_down[...], NT, preferred_element_type=F32)
            two = mask_keep[2 * x2, 2 * y2:2 * y2 + 2] + mask_keep[2 * x2 + 1, 2 * y2:2 * y2 + 2]
            four = jnp.broadcast_to(jnp.sum(two, axis=0, keepdims=True), (cc, zl)).astype(BF)
            on = lax.dot_general(spread, four, NT, preferred_element_type=F32)
            on_keep[x2, y2] = on
            v = silu(lifted * gains + shifts)
            coarse[1 + x2, 1 + y2] = jnp.where(on > 0, v, 0.0).astype(BF)

    send(2, coarse)
    inner(decode_enc)
    loads[10].wait()
    arrive(2, coarse)
    send(1, enc)

    halves = cx

    @pl.loop(0, cx // halves)
    def _(x2):
        x2 = x2 * halves
        taps, weights = [], []
        for a in range(3):
            for b in range(3):
                taps.append(coarse[pl.ds(x2 + a, halves), b:b + cy].reshape(halves * cy * kz, cc))
                tap = 9 * a + 3 * b
                weights.append(w_coarse_ref[tap:tap + 3].reshape(3 * cc, cc))
        r = lax.dot_general(jnp.concatenate(taps, axis=1), jnp.concatenate(weights, axis=1), NT,
                            preferred_element_type=F32)
        n = halves * cy * kz
        v = pltpu.roll(r[:, 0:cc], 1, 0) + r[:, cc:2 * cc] + pltpu.roll(r[:, 2 * cc:], n - 1, 0)
        on = on_keep[pl.ds(x2, halves)].reshape(n, cc)
        act = jnp.where(on > 0, silu(v + b_coarse), 0.0).astype(BF)
        up = lax.dot_general(act, w_up_ref[...], NT, preferred_element_type=F32).astype(BF)
        for h in range(halves):
            for y2 in range(cy):
                at = (h * cy + y2) * kz
                flat[x2 + h, :, y2 * chans:(y2 + 1) * chans] = up[at:at + kz]

    def raise_z(columns, count):
        wide = lax.dot_general(columns, spread, TN, preferred_element_type=F32)
        return wide.astype(BF).reshape(count, chans, zl)

    for x2 in range(cx):
        for at, y2 in enumerate((0, cy - 1)):
            y_out[at, :, x2 * chans:(x2 + 1) * chans] = flat[x2, :, y2 * chans:(y2 + 1) * chans]
        lift[1 + x2, 1:1 + cy] = raise_z(flat[x2], cy)
    send(3, lift)
    arrive(1, enc)
    outer(decode_enc)

    arrive(3, lift)
    for at, edge_at in enumerate((0, cx + 1)):
        lift[edge_at, 1:1 + cy] = raise_z(side_x[at], cy)
    for at, edge_at in enumerate((0, cy + 1)):
        lift[1:1 + cx, edge_at] = raise_z(side_y[at], cx)

    @pl.loop(0, cx)
    def _(x2):
        for y0 in range(0, ty, 2):
            part = acc[x2, y0 // 2] + jnp.dot(
                k_dec_l[...], gather_lift(x2, y0), preferred_element_type=F32)
            for dx in range(2):
                for dy in range(2):
                    v = fold(part, dx, dy) + b_dec
                    turn[2 * x2 + dx, pl.ds(y0 + dy, chans, stride=ty), :] = v
        for dx in range(2):
            tile = turn[2 * x2 + dx].reshape(chans, ty, zl)[:, :, 0:tz]
            tile = jnp.where(mask_ref[2 * x2 + dx][None] > 0, tile, 0.0)
            out_ref[:, 2 * x2 + dx] = tile.astype(BF)

    for phase, buf in enumerate((masked, enc, coarse, lift)):
        sent(phase, buf)


def on_device(n_narrow, n_wide, fine_in, voxel_mask, timestep, w_enc, b_enc, w_down, w_time,
              w_coarse, b_coarse, w_up, w_dec, b_dec):
    chans, tx, ty, tz = fine_in.shape
    cc = w_down.shape[0]
    zl = round_up(tz + 1, LANES)
    kz = round_up(tz // 2 + 1, 16)
    inputs = (fine_in, voxel_mask, w_enc, w_down, w_dec, w_time, b_enc[None], b_dec[None],
              b_coarse[None], w_up, w_coarse)
    k_rows, k_cols = 6 * chans, 12 * chans
    vmem = pl.BlockSpec(memory_space=pltpu.VMEM)
    return pl.pallas_call(
        functools.partial(fine_kernel, n_narrow, n_wide),
        out_shape=pltpu.VMEM(fine_in.shape, BF),
        in_specs=[pl.BlockSpec(memory_space=pltpu.SMEM)]
        + [pl.BlockSpec(memory_space=pltpu.HBM)] * len(inputs),
        out_specs=vmem,
        scratch_shapes=[pltpu.VMEM(a.shape, a.dtype) for a in inputs] + [
            pltpu.VMEM((tx + 2, ty + 2, chans, zl), BF),
            pltpu.VMEM((tx + 2, ty + 2, chans, zl), BF),
            pltpu.VMEM((tx // 2 + 2, ty // 2 + 2, kz, cc), BF),
            pltpu.VMEM((tx // 2 + 2, ty // 2 + 2, chans, zl), BF),
            pltpu.VMEM((tx // 2, kz, ty // 2 * chans), BF),
            pltpu.VMEM((2, kz, tx // 2 * chans), BF),
            pltpu.VMEM((2, kz, ty // 2 * chans), BF),
            pltpu.VMEM((2, kz, tx // 2 * chans), BF),
            pltpu.VMEM((tx // 2, ty // 2, kz, cc), F32),
            pltpu.VMEM((tx, ty, zl), F32),
            pltpu.VMEM((tx, chans * ty, zl), F32),
            pltpu.VMEM((tx // 2, ty // 2, k_rows, 2 * zl), F32),
            pltpu.VMEM((k_rows, k_cols), BF),
            pltpu.VMEM((k_rows, k_cols), BF),
            pltpu.VMEM((k_rows, k_cols), BF),
            pltpu.VMEM((cc, 8 * chans), BF),
            pltpu.SemaphoreType.DMA((4, len(WAYS))),
            pltpu.SemaphoreType.DMA((4, len(WAYS))),
            pltpu.SemaphoreType.DMA((len(inputs),)),
        ],
        compiler_params=pltpu.CompilerParams(
            collective_id=0, has_side_effects=True, vmem_limit_bytes=63 * 1024 * 1024
        ),
    )(timestep, *inputs)


def solution(mesh):
    return jax.shard_map(
        functools.partial(on_device, mesh.shape["narrow"], mesh.shape["wide"]),
        mesh=mesh,
        in_specs=(
            P(None, "narrow", "wide", None),
            P("narrow", "wide", None),
            P(), P(), P(), P(), P(), P(), P(), P(), P(), P(),
        ),
        out_specs=P(None, "narrow", "wide", None),
        check_vma=False,
    )
```
